256 devices in a mesh: tensor: 4 (over y_hi, core), dp: 64 (over z, y_lo, x).
Axes of the slice: x: 4, y: 4 (y_hi: 2, y_lo: 2; y = y_hi * 2 + y_lo), z: 8, core: 2. Of those that a mesh axis runs over, the one named last changes fastest.
Arguments:
- attn_out: bfloat16 [32768, 4096], P('dp', 'tensor'), may hold values from -6 to 6
- out_grad: bfloat16 [32768, 4096], P('dp', 'tensor'), may hold values from -0.21875 to 0.21875
- q_left: bfloat16 [4, 4, 1024, 1024], P('tensor', None, 'dp'), may hold values from -0.1875 to 0.1875
- q_right: bfloat16 [4, 1024, 1024], P('tensor', 'dp'), may hold values from -0.1875 to 0.1875
- weight: float32 [4096, 4096], P('dp', 'tensor'), may hold values from -6 to 6
- moment: float32 [4096, 4096], P(('tensor', 'dp')), may hold values from -6 to 6
- second: float32 [4096, 4096], P(('tensor', 'dp')), may hold values from 0.25 to 4
Outputs:
- new_weight: float32 [4096, 4096], P('dp', 'tensor')
- update: bfloat16 [4096, 4096], P('dp', 'tensor')
- new_moment: float32 [4096, 4096], P(('tensor', 'dp'))
- new_second: float32 [4096, 4096], P(('tensor', 'dp'))
The draws below stay inside these ranges and needn't reach their ends.
All inputs are finite; a program needn't handle non-finite values.
Results may differ from the reference program's by a relative error of at most 0.001.
Values may be sent and summed in bfloat16 or wider, within the bound.
No kernel may reach another device: no remote copies, remote signals or barrier semaphores. Data moves between devices by JAX's collectives and lax.ppermute only.
A program may use at most 128 MiB of HBM per device.

```python
import math
import jax
import jax.numpy as jnp
from jax import lax

BLK = 1024
NB = 4
STEP = 10
TOK_DEV = 512
IN_TP = 1024
IN_ALL = 4096
OUT = 4096
TOKENS = 32768
N_TENSOR = 4
N_DP = 64


def raised(result, rng, source, target, shards_of, factor):
    owner, partner = [(jnp.arange(result.shape[dim]) // (result.shape[dim] // shards_of)).reshape([-1 if axis == dim else 1 for axis in range(result.ndim)]) for dim in (source, target)]
    chosen = jax.random.permutation(rng, shards_of)[partner]
    strong = (owner == chosen) | (owner == (partner + shards_of // 2) % shards_of)
    return jnp.where(strong, factor * result, result)


def levels(stream_key, dims, split, low, high):
    def one(axis_at, parts):
        draws = jax.random.uniform(jax.random.fold_in(jax.random.fold_in(stream_key, 6), axis_at), (parts,), jnp.float32, low / len(split), high / len(split))
        return jnp.repeat(jnp.exp(draws), dims[axis_at] // parts).reshape((-1,) + (1,) * (len(dims) - axis_at - 1))

    level = one(*split[0])
    for cut in split[1:]:
        level = level * one(*cut)
    return level


def centred(key, dims, deviation, bound, split=(), dtype=jnp.bfloat16):
    drawn = jax.random.normal(key, dims, jnp.float32) * deviation
    if len(split) > 0:
        drawn = levels(key, dims, split, -0.22, 0.18) * drawn
    return jnp.clip(drawn, min=-bound, max=bound).astype(dtype)


def gaussian_with(key, extent, deviation, reach, pieces, heavy, held_as=jnp.bfloat16):
    array = deviation * jax.random.normal(key, extent, jnp.float32)
    if pieces:
        array = array * levels(key, extent, pieces, -0.22, 0.18)
    return jnp.clip(raised(array, jax.random.fold_in(key, 3), *heavy), -reach, reach).astype(held_as)


def setup_inputs(seed: int = 0) -> dict:
    keys = jax.random.split(jax.random.key(seed), 8)
    attn_out = centred(keys[0], (TOKENS, IN_ALL), 1.0, 6.0, ((0, 64), (1, 4)))
    out_grad = gaussian_with(keys[1], (TOKENS, OUT), (1.0 / (TOK_DEV * N_DP) ** 0.5), 0.21875, ((0, 64), (1, 4)), (0, 1, 64, 4.0))
    q_left = centred(keys[2], (N_TENSOR, NB, BLK, BLK), BLK ** -0.5, 0.1875, ((0, 4), (2, 64)))
    q_right = centred(keys[3], (N_TENSOR, BLK, BLK), BLK ** -0.5, 0.1875, ((0, 4), (1, 64)))
    weight = centred(keys[4], (OUT, IN_ALL), 1.0, 6.0, ((0, 64), (1, 4)), jnp.float32)
    moment = centred(keys[5], (IN_ALL, OUT), 1.0, 6.0, ((0, 256),), jnp.float32)
    second = jnp.clip(jnp.exp(math.log(4.0) - 2.7725887 * jax.random.uniform(keys[6], (IN_ALL, OUT), jnp.float32) ** levels(keys[6], (IN_ALL, OUT), ((0, 256),), -0.2, 0.2)), 0.25, 4.0)
    return dict(attn_out=attn_out, out_grad=out_grad, q_left=q_left, q_right=q_right, weight=weight, moment=moment, second=second)


beta_first = 0.9
beta_second = 0.95
adam_eps = 1e-08
learn_rate = 0.1
weight_decay = 0.1

def adam_step(moment, second, rotated):
    new_moment = beta_first * moment + (1.0 - beta_first) * rotated
    new_second = beta_second * second + (1.0 - beta_second) * rotated * rotated
    first_fix = 1.0 - beta_first ** STEP
    second_fix = 1.0 - beta_second ** STEP
    normed = new_moment / first_fix / (jnp.sqrt(new_second / second_fix) + adam_eps)
    return (new_moment, new_second, normed)

def reference(attn_out, out_grad, q_left, q_right, weight, moment, second):
    grad = jnp.dot(out_grad.T, attn_out, preferred_element_type=jnp.float32)
    weight_parts, update_parts, moment_parts, second_parts = ([], [], [], [])
    for tensor_index in range(N_TENSOR):
        column_start = tensor_index * IN_TP
        shard_grad = grad[:, column_start:column_start + IN_TP]
        left_basis = q_left[tensor_index].astype(jnp.float32)
        right_basis = q_right[tensor_index].astype(jnp.float32)
        turned = jnp.dot(shard_grad, right_basis, precision=lax.Precision.HIGHEST)
        rotated = jnp.einsum('bop,boi->ibp', left_basis, turned.reshape(NB, BLK, IN_TP), precision=lax.Precision.HIGHEST).reshape(IN_TP, OUT)
        new_moment, new_second, normed = adam_step(moment[column_start:column_start + IN_TP], second[column_start:column_start + IN_TP], rotated)
        back_left = jnp.einsum('ibp,bop->ibo', normed.reshape(IN_TP, NB, BLK), left_basis, precision=lax.Precision.HIGHEST).reshape(IN_TP, OUT)
        unrotated = jnp.dot(back_left.T, right_basis.T, precision=lax.Precision.HIGHEST)
        weight_part = weight[:, column_start:column_start + IN_TP]
        weight_parts.append(weight_part - learn_rate * (unrotated + weight_decay * weight_part))
        update_parts.append(unrotated.astype(jnp.bfloat16))
        moment_parts.append(new_moment)
        second_parts.append(new_second)
    return (jnp.concatenate(weight_parts, axis=1), jnp.concatenate(update_parts, axis=1), jnp.concatenate(moment_parts, axis=0), jnp.concatenate(second_parts, axis=0))
```

```python
import jax
import jax.numpy as jnp
from jax import lax
from jax.sharding import Mesh, PartitionSpec as P

STEP = 10


beta_first = 0.9
beta_second = 0.95
adam_eps = 1e-08
learn_rate = 0.1
weight_decay = 0.1

SIZES = {"yh": 2, "core": 2, "zh": 4, "zl": 2, "yl": 2, "x": 4}
Z = ("zh", "zl")
F32, BF16 = jnp.float32, jnp.bfloat16


def adam_step(moment, second, rotated):
    new_moment = beta_first * moment + (1.0 - beta_first) * rotated
    new_second = beta_second * second + (1.0 - beta_second) * rotated * rotated
    first_fix = 1.0 - beta_first**STEP
    second_fix = 1.0 - beta_second**STEP
    normed = new_moment / first_fix / (jnp.sqrt(new_second / second_fix) + adam_eps)
    return (new_moment, new_second, normed)


def shift(value, axes, count, by):
    return lax.ppermute(value, axes, [(i, (i + by) % count) for i in range(count)])


def swap(value, axis):
    return shift(value, axis, 2, 1)


def split(value, dim):
    high = lax.reduce_precision(value, 8, 7)
    low = value - high
    return jnp.concatenate([high.astype(BF16), low.astype(BF16)], axis=dim)


def fold(value):
    half = value.shape[0] // 2
    return value[:half] + value[half:]


def dot(left, right, left_dim, right_dim):
    return lax.dot_general(
        left, right, (((left_dim,), (right_dim,)), ((), ())), preferred_element_type=F32
    )


def ring_sum(parts, axes, count, dim, up):
    here = lax.axis_index(axes)

    def block(offset):
        return lax.dynamic_index_in_dim(parts, (here + offset) % count, dim, keepdims=False)

    down = count - 1 - up
    from_below, from_above = block(up), block(-down)
    for step in range(max(up, down)):
        if step < up:
            from_below = shift(from_below, axes, count, 1)
            if step < up - 1:
                from_below = from_below + block(up - 1 - step)
        if step < down:
            from_above = shift(from_above, axes, count, -1)
            if step < down - 1:
                from_above = from_above + block(-(down - 1 - step))
    return block(0) + from_below + from_above


def local(attn_out, out_grad, q_left, q_right, weight, moment, second):
    yl, yh, core = (lax.axis_index(a) for a in ("yl", "yh", "core"))

    grad_1 = swap(out_grad, "core")
    half = out_grad.shape[1] // 2
    mine = lax.dynamic_slice_in_dim(out_grad, yl * half, half, 1)
    others = lax.dynamic_slice_in_dim(out_grad, (1 - yl) * half, half, 1)
    grad_2 = swap(mine, "yh")
    grad_2y = lax.ppermute(others, ("yh", "yl"), [(i, 3 - i) for i in range(4)])
    attn_y = swap(attn_out, "yl")
    grad_3, grad_3y = swap(grad_2, "core"), swap(grad_2y, "core")

    part_0 = dot(out_grad, attn_out, 0, 0).reshape(2, 4, 128, 1024)
    part_1 = dot(grad_1, attn_out, 0, 0).reshape(2, 4, 128, 1024)
    sum_0 = ring_sum(part_0, "x", 4, 1, 2)
    sum_1 = ring_sum(part_1, "x", 4, 1, 1)
    both = jnp.stack([sum_0, sum_1]).reshape(2, 2, 8, 16, 1024)
    both = ring_sum(both, Z, 8, 2, 4)
    kept = lax.dynamic_index_in_dim(both, yl, 1, keepdims=False)
    given = lax.dynamic_index_in_dim(both, 1 - yl, 1, keepdims=False)
    rows_a = kept + swap(given, "yl")

    part_2 = dot(grad_2, attn_out, 0, 0) + dot(grad_2y, attn_y, 0, 0)
    part_3 = dot(grad_3, attn_out, 0, 0) + dot(grad_3y, attn_y, 0, 0)
    part_b = jnp.stack([part_2, part_3]).reshape(2, 4, 8, 16, 1024)
    rows_b = ring_sum(part_b, Z, 8, 2, 3)
    rows_b = ring_sum(rows_b, "x", 4, 1, 2)
    rows = jnp.concatenate([rows_a, rows_b]).reshape(64, 1024)

    right = q_right[0].reshape(16, 4, 16, 16).transpose(0, 2, 1, 3).reshape(16, 1024)
    right = lax.all_gather(right, ("yl", "x"), axis=0, tiled=True)
    right = lax.all_gather(right, Z, axis=0, tiled=True)
    left = lax.all_to_all(q_left[0], "zh", 0, 0, tiled=True)
    left = lax.all_gather(left, "x", axis=0)
    left = lax.all_gather(left, ("zl", "yl"), axis=0)
    left = left.reshape(16, 4, 16, 1024).transpose(1, 0, 2, 3).reshape(1024, 1024)

    def to_block(value):
        moved = value.reshape(16, 4, 1024).transpose(1, 0, 2)
        return lax.all_to_all(moved, "zh", 0, 0, tiled=True).reshape(64, 1024)

    moment_b, second_b = to_block(moment), to_block(second)

    turned = fold(dot(split(rows, 0), right, 1, 0)).reshape(4, 16, 2, 2, 4, 64)
    turned = jnp.where(core == 1, turned[jnp.array([1, 0, 3, 2])], turned)
    turned = jnp.where(yh == 1, turned[jnp.array([2, 3, 0, 1])], turned)
    turned = turned.transpose(3, 4, 0, 2, 1, 5).reshape(64, 16, 64)
    turned = lax.all_to_all(turned, ("yl", "x", "zh", "zl"), 0, 0, tiled=True).reshape(1024, 64)
    rotated = fold(dot(split(turned, 1), left, 0, 0))
    normed = adam_step(moment_b, second_b, rotated)[2]
    back = fold(dot(split(normed, 0), left, 1, 1)).reshape(64, 16, 64).transpose(1, 0, 2)
    back = lax.all_to_all(back, ("zl", "yl", "x"), 0, 0, tiled=True).reshape(1024, 64)
    unrotated = fold(dot(split(back, 1), right, 0, 1))

    own = lax.all_to_all(rotated.reshape(4, 16, 1024), "zh", 0, 0, tiled=True)
    own = own.transpose(1, 0, 2).reshape(16, 4096)
    new_moment, new_second, _ = adam_step(moment, second, own)
    new_weight = weight - learn_rate * (unrotated + weight_decay * weight)
    return (new_weight, unrotated.astype(BF16), new_moment, new_second)


def solution(mesh):
    fine = Mesh(mesh.devices.reshape(tuple(SIZES.values())), tuple(SIZES))
    tensor, dp = ("yh", "core"), ("zh", "zl", "yl", "x")
    whole = tensor + dp
    return jax.shard_map(
        local,
        mesh=fine,
        in_specs=(
            P(dp, tensor),
            P(dp, tensor),
            P(tensor, None, dp, None),
            P(tensor, dp, None),
            P(dp, tensor),
            P(whole, None),
            P(whole, None),
        ),
        out_specs=(P(dp, tensor), P(dp, tensor), P(whole, None), P(whole, None)),
        check_vma=False,
    )
```

```python
import jax
import jax.numpy as jnp
from jax import lax
from jax.sharding import Mesh, PartitionSpec as P

STEP = 10


beta_first = 0.9
beta_second = 0.95
adam_eps = 1e-08
learn_rate = 0.1
weight_decay = 0.1

SIZES = {"yh": 2, "core": 2, "zh": 4, "zl": 2, "yl": 2, "x": 4}
Z = ("zh", "zl")
F32, BF16 = jnp.float32, jnp.bfloat16


def adam_step(moment, second, rotated):
    new_moment = beta_first * moment + (1.0 - beta_first) * rotated
    new_second = beta_second * second + (1.0 - beta_second) * rotated * rotated
    first_fix = 1.0 - beta_first**STEP
    second_fix = 1.0 - beta_second**STEP
    normed = new_moment / first_fix / (jnp.sqrt(new_second / second_fix) + adam_eps)
    return (new_moment, new_second, normed)


def shift(value, axes, count, by):
    return lax.ppermute(value, axes, [(i, (i + by) % count) for i in range(count)])


def swap(value, axis):
    return shift(value, axis, 2, 1)


def split(value, dim):
    high = lax.reduce_precision(value, 8, 7)
    low = value - high
    return jnp.concatenate([high.astype(BF16), low.astype(BF16)], axis=dim)


def fold(value):
    half = value.shape[0] // 2
    return value[:half] + value[half:]


def dot(left, right, left_dim, right_dim):
    return lax.dot_general(
        left, right, (((left_dim,), (right_dim,)), ((), ())), preferred_element_type=F32
    )


def ring_sum(parts, axes, count, dim, up):
    here = lax.axis_index(axes)

    def block(offset):
        return lax.dynamic_index_in_dim(parts, (here + offset) % count, dim, keepdims=False)

    down = count - 1 - up
    from_below, from_above = block(up), block(-down)
    for step in range(max(up, down)):
        if step < up:
            from_below = shift(from_below, axes, count, 1)
            if step < up - 1:
                from_below = from_below + block(up - 1 - step)
        if step < down:
            from_above = shift(from_above, axes, count, -1)
            if step < down - 1:
                from_above = from_above + block(-(down - 1 - step))
    return block(0) + from_below + from_above


def local(attn_out, out_grad, q_left, q_right, weight, moment, second):
    yl, yh, core = (lax.axis_index(a) for a in ("yl", "yh", "core"))

    grad_1 = swap(out_grad, "core")
    part_0 = dot(out_grad, attn_out, 0, 0).reshape(2, 4, 128, 1024)
    part_1 = dot(grad_1, attn_out, 0, 0).reshape(2, 4, 8, 16, 1024)
    sum_0 = ring_sum(part_0, "x", 4, 1, 2).reshape(2, 8, 16, 1024)
    sum_1 = ring_sum(part_1, Z, 8, 2, 4)

    right = q_right[0].reshape(16, 4, 16, 16).transpose(0, 2, 1, 3).reshape(1, 16, 1024)
    bases = jnp.concatenate([q_left[0], jnp.broadcast_to(right, (4, 16, 1024))], axis=1)
    late_grad, late_attn, bases, _ = lax.optimization_barrier((out_grad, attn_out, bases, part_1))
    bases = lax.all_to_all(bases, "zh", 0, 0, tiled=True)
    moved = jnp.stack([moment, second]).reshape(2, 16, 4, 1024).transpose(2, 0, 1, 3)
    bases, moved = lax.optimization_barrier((bases, moved))
    moved = lax.all_to_all(moved, "zh", 0, 0, tiled=True)
    bases = lax.all_gather(bases, ("zl", "yl", "x"), axis=0)
    bases = bases.reshape(16, 4, 2, 16, 1024).transpose(2, 1, 0, 3, 4).reshape(2, 1024, 1024)
    left, right = bases[0], bases[1]

    half = out_grad.shape[1] // 2
    mine = lax.dynamic_slice_in_dim(late_grad, yl * half, half, 1)
    others = lax.dynamic_slice_in_dim(late_grad, (1 - yl) * half, half, 1)
    grad_2 = swap(mine, "yh")
    grad_2y = lax.ppermute(others, ("yh", "yl"), [(i, 3 - i) for i in range(4)])
    attn_y = swap(late_attn, "yl")
    grad_3, grad_3y = swap(grad_2, "core"), swap(grad_2y, "core")
    part_2 = dot(grad_2, attn_out, 0, 0) + dot(grad_2y, attn_y, 0, 0)
    part_3 = dot(grad_3, attn_out, 0, 0) + dot(grad_3y, attn_y, 0, 0)
    sum_2 = ring_sum(part_2.reshape(4, 128, 1024), "x", 4, 0, 2)
    sum_3 = ring_sum(part_3.reshape(4, 128, 1024), "x", 4, 0, 1)

    sum_0 = ring_sum(sum_0, Z, 8, 1, 3)
    sum_1 = ring_sum(sum_1, "x", 4, 1, 1)
    both = jnp.stack([sum_0, sum_1])
    kept = lax.dynamic_index_in_dim(both, yl, 1, keepdims=False)
    given = lax.dynamic_index_in_dim(both, 1 - yl, 1, keepdims=False)
    rows_a = kept + swap(given, "yl")

    rows_b = jnp.stack([sum_2, sum_3])
    rows_b, moved = lax.optimization_barrier((rows_b, moved))
    moment_b, second_b = (moved[:, i].reshape(64, 1024) for i in (0, 1))
    rows_b = ring_sum(rows_b.reshape(2, 8, 16, 1024), Z, 8, 1, 4)
    rows_a = jnp.where(core == 1, rows_a[::-1], rows_a)
    rows_b = jnp.where(core == 1, rows_b[::-1], rows_b)
    rows = jnp.concatenate(
        [jnp.where(yh == 1, rows_b, rows_a), jnp.where(yh == 1, rows_a, rows_b)]
    ).reshape(64, 1024)

    turned = fold(dot(split(rows, 0), right, 1, 0)).reshape(4, 16, 2, 2, 4, 64)
    turned = turned.transpose(3, 4, 0, 2, 1, 5).reshape(64, 16, 64)
    turned = lax.all_to_all(turned, ("yl", "x", "zh", "zl"), 0, 0, tiled=True).reshape(1024, 64)
    rotated = fold(dot(split(turned, 1), left, 0, 0))
    normed = adam_step(moment_b, second_b, rotated)[2]
    back = fold(dot(split(normed, 0), left, 1, 1)).reshape(64, 16, 64).transpose(1, 0, 2)
    back, rotated = lax.optimization_barrier((back, rotated))
    back = lax.all_to_all(back, ("zl", "yl", "x"), 0, 0, tiled=True).reshape(1024, 64)
    unrotated = fold(dot(split(back, 1), right, 0, 1))

    zh = lax.axis_index("zh")
    tiles = rotated.reshape(4, 16, 1024)
    own = jnp.zeros((4, 16, 1024), F32)
    for step in range(4):
        sent = lax.dynamic_index_in_dim(tiles, (zh + step) % 4, 0, keepdims=False)
        got = shift(sent, "zh", 4, step) if step else sent
        own = lax.dynamic_update_index_in_dim(own, got, (zh - step) % 4, 0)
    own = own.transpose(1, 0, 2).reshape(16, 4096)
    new_moment, new_second, _ = adam_step(moment, second, own)
    new_weight = weight - learn_rate * (unrotated + weight_decay * weight)
    return (new_weight, unrotated.astype(BF16), new_moment, new_second)


def solution(mesh):
    fine = Mesh(mesh.devices.reshape(tuple(SIZES.values())), tuple(SIZES))
    tensor, dp = ("yh", "core"), ("zh", "zl", "yl", "x")
    whole = tensor + dp
    return jax.shard_map(
        local,
        mesh=fine,
        in_specs=(
            P(dp, tensor),
            P(dp, tensor),
            P(tensor, None, dp, None),
            P(tensor, dp, None),
            P(dp, tensor),
            P(whole, None),
            P(whole, None),
        ),
        out_specs=(P(dp, tensor), P(dp, tensor), P(whole, None), P(whole, None)),
        check_vma=False,
    )
```

```python
import jax
import jax.numpy as jnp
from jax import lax
from jax.sharding import Mesh, PartitionSpec as P

STEP = 10


beta_first = 0.9
beta_second = 0.95
adam_eps = 1e-08
learn_rate = 0.1
weight_decay = 0.1

SIZES = {"yh": 2, "core": 2, "zh": 4, "zl": 2, "yl": 2, "x": 4}
Z = ("zh", "zl")
F32, BF16 = jnp.float32, jnp.bfloat16


def adam_step(moment, second, rotated):
    new_moment = beta_first * moment + (1.0 - beta_first) * rotated
    new_second = beta_second * second + (1.0 - beta_second) * rotated * rotated
    first_fix = 1.0 - beta_first**STEP
    second_fix = 1.0 - beta_second**STEP
    normed = new_moment / first_fix / (jnp.sqrt(new_second / second_fix) + adam_eps)
    return (new_moment, new_second, normed)


def shift(value, axes, count, by):
    return lax.ppermute(value, axes, [(i, (i + by) % count) for i in range(count)])


def swap(value, axis):
    return shift(value, axis, 2, 1)


def pair(value, axis):
    other, first = swap(value, axis), lax.axis_index(axis) == 0
    return jnp.stack([jnp.where(first, value, other), jnp.where(first, other, value)])


def split(value, dim):
    high = lax.reduce_precision(value, 8, 7)
    low = value - high
    return jnp.concatenate([high.astype(BF16), low.astype(BF16)], axis=dim)


def fold(value):
    half = value.shape[0] // 2
    return value[:half] + value[half:]


def dot(left, right, left_dim, right_dim):
    return lax.dot_general(
        left, right, (((left_dim,), (right_dim,)), ((), ())), preferred_element_type=F32
    )


def after(values, earlier):
    return lax.optimization_barrier((values, earlier))[0]


def ring_sum(parts, axes, count, dim, up, seen=None):
    here = lax.axis_index(axes)

    def block(offset):
        return lax.dynamic_index_in_dim(parts, (here + offset) % count, dim, keepdims=False)

    down = count - 1 - up
    from_below, from_above = block(up), block(-down)
    for step in range(max(up, down)):
        if step < up:
            from_below = shift(from_below, axes, count, 1)
            if step < up - 1:
                from_below = from_below + block(up - 1 - step)
                if seen is not None:
                    seen.append(from_below)
        if step < down:
            from_above = shift(from_above, axes, count, -1)
            if step < down - 1:
                from_above = from_above + block(-(down - 1 - step))
    return block(0) + from_below + from_above if down else block(0) + from_below


def local(attn_out, out_grad, q_left, q_right, weight, moment, second):
    yl, yh, core = (lax.axis_index(a) for a in ("yl", "yh", "core"))

    half = out_grad.shape[1] // 2
    mine = lax.dynamic_slice_in_dim(out_grad, yl * half, half, 1)
    others = lax.dynamic_slice_in_dim(out_grad, (1 - yl) * half, half, 1)
    grad_1 = swap(out_grad, "core")
    grad_2 = swap(mine, "yh")
    grad_2y = lax.ppermute(others, ("yh", "yl"), [(i, 3 - i) for i in range(4)])
    attn_y = swap(attn_out, "yl")

    part_0 = dot(out_grad, attn_out, 0, 0).reshape(2, 4, 128, 1024)
    part_1 = dot(grad_1, attn_out, 0, 0).reshape(2, 4, 8, 16, 1024)
    seen_0, seen_1 = [], []
    sum_0 = ring_sum(part_0, "x", 4, 1, 2, seen_0).reshape(2, 8, 16, 1024)
    sum_1 = ring_sum(part_1, Z, 8, 2, 4, seen_1)

    right = q_right[0].reshape(16, 4, 16, 16).transpose(0, 2, 1, 3).reshape(1, 16, 1024)
    bases = jnp.concatenate([q_left[0], jnp.broadcast_to(right, (4, 16, 1024))], axis=1)
    bases = lax.all_to_all(after(bases, part_1), "zh", 0, 0, tiled=True)
    moved = jnp.stack([moment, second]).reshape(2, 16, 4, 1024).transpose(2, 0, 1, 3)
    moved = lax.all_to_all(after(moved, bases), "zh", 0, 0, tiled=True)
    bases = pair(bases, "zl")
    bases = lax.all_gather(bases, "x", axis=0).reshape(4, 2, 4, 2, 16, 1024)
    right = pair(bases[:, :, :, 1], "yl")
    left = pair(after(bases[:, :, :, 0], right), "yl")

    grad_2, grad_2y, attn_y = after((grad_2, grad_2y, attn_y), (seen_0[0], seen_1[0]))
    grad_3, grad_3y = swap(grad_2, "core"), swap(grad_2y, "core")
    part_2 = dot(grad_2, attn_out, 0, 0) + dot(grad_2y, attn_y, 0, 0)
    part_3 = dot(grad_3, attn_out, 0, 0) + dot(grad_3y, attn_y, 0, 0)
    sum_2 = ring_sum(part_2.reshape(4, 128, 1024), "x", 4, 0, 2)
    sum_3 = ring_sum(part_3.reshape(4, 128, 1024), "x", 4, 0, 1)

    sum_0 = ring_sum(sum_0, "yl", 2, 0, 1)
    sum_1 = ring_sum(ring_sum(sum_1, "yl", 2, 0, 1), "x", 4, 0, 1)
    rest = jnp.stack([sum_0.reshape(128, 1024), sum_2, sum_3]).reshape(3, 8, 16, 1024)
    rest, moved, right = lax.optimization_barrier((rest, moved, right))
    right, left = (b.transpose(3, 2, 0, 1, 4, 5).reshape(1024, 1024) for b in (right, left))
    moment_b, second_b = (moved[:, i].reshape(64, 1024) for i in (0, 1))
    row_0, row_2, row_3 = ring_sum(rest, Z, 8, 1, 4)
    rows_a, rows_b = jnp.stack([row_0, sum_1]), jnp.stack([row_2, row_3])
    rows_a = jnp.where(core == 1, rows_a[::-1], rows_a)
    rows_b = jnp.where(core == 1, rows_b[::-1], rows_b)
    rows = jnp.concatenate(
        [jnp.where(yh == 1, rows_b, rows_a), jnp.where(yh == 1, rows_a, rows_b)]
    ).reshape(64, 1024)

    turned = fold(dot(split(rows, 0), right, 1, 0)).reshape(4, 16, 2, 2, 4, 64)
    turned = turned.transpose(3, 4, 0, 2, 1, 5).reshape(64, 16, 64)
    turned = lax.all_to_all(turned, ("yl", "x", "zh", "zl"), 0, 0, tiled=True).reshape(1024, 64)
    rotated = fold(dot(split(turned, 1), left, 0, 0))
    normed = adam_step(moment_b, second_b, rotated)[2]
    back = fold(dot(split(normed, 0), left, 1, 1)).reshape(64, 16, 64).transpose(1, 0, 2)
    back, rotated = lax.optimization_barrier((back, rotated))
    back = lax.all_to_all(back, ("zl", "yl", "x"), 0, 0, tiled=True).reshape(1024, 64)
    unrotated = fold(dot(split(back, 1), right, 0, 1))

    zh = lax.axis_index("zh")
    tiles = rotated.reshape(4, 16, 1024)
    own = jnp.zeros((4, 16, 1024), F32)
    for step in range(4):
        sent = lax.dynamic_index_in_dim(tiles, (zh + step) % 4, 0, keepdims=False)
        got = shift(sent, "zh", 4, step) if step else sent
        own = lax.dynamic_update_index_in_dim(own, got, (zh - step) % 4, 0)
    own = own.transpose(1, 0, 2).reshape(16, 4096)
    new_moment, new_second, _ = adam_step(moment, second, own)
    new_weight = weight - learn_rate * (unrotated + weight_decay * weight)
    return (new_weight, unrotated.astype(BF16), new_moment, new_second)


def solution(mesh):
    fine = Mesh(mesh.devices.reshape(tuple(SIZES.values())), tuple(SIZES))
    tensor, dp = ("yh", "core"), ("zh", "zl", "yl", "x")
    whole = tensor + dp
    return jax.shard_map(
        local,
        mesh=fine,
        in_specs=(
            P(dp, tensor),
            P(dp, tensor),
            P(tensor, None, dp, None),
            P(tensor, dp, None),
            P(dp, tensor),
            P(whole, None),
            P(whole, None),
        ),
        out_specs=(P(dp, tensor), P(dp, tensor), P(whole, None), P(whole, None)),
        check_vma=False,
    )
```

```python
import jax
import jax.numpy as jnp
from jax import lax
from jax.experimental import pallas as pl
from jax.experimental.pallas import tpu as pltpu
from jax.sharding import Mesh, PartitionSpec as P

STEP = 10


beta_first = 0.9
beta_second = 0.95
adam_eps = 1e-08
learn_rate = 0.1
weight_decay = 0.1

SIZES = {"yh": 2, "core": 2, "zh": 4, "zl": 2, "yl": 2, "x": 4}
Z = ("zh", "zl")
F32, BF16 = jnp.float32, jnp.bfloat16


def adam_step(moment, second, rotated):
    new_moment = beta_first * moment + (1.0 - beta_first) * rotated
    new_second = beta_second * second + (1.0 - beta_second) * rotated * rotated
    first_fix = 1.0 - beta_first**STEP
    second_fix = 1.0 - beta_second**STEP
    normed = new_moment / first_fix / (jnp.sqrt(new_second / second_fix) + adam_eps)
    return (new_moment, new_second, normed)


def shift(value, axes, count, by):
    return lax.ppermute(value, axes, [(i, (i + by) % count) for i in range(count)])


def swap(value, axis):
    return shift(value, axis, 2, 1)


def pair(value, axis):
    other, first = swap(value, axis), lax.axis_index(axis) == 0
    return jnp.stack([jnp.where(first, value, other), jnp.where(first, other, value)])


def split(value, dim):
    high = value.astype(BF16)
    low = (value - high.astype(F32)).astype(BF16)
    return jnp.concatenate([high, low], axis=dim)


def fold(value):
    half = value.shape[0] // 2
    return value[:half] + value[half:]


def dot(left, right, left_dim, right_dim):
    return lax.dot_general(
        left, right, (((left_dim,), (right_dim,)), ((), ())), preferred_element_type=F32
    )


def pack(value):
    half = value.shape[0] // 2
    return jnp.concatenate([value[:half], value[half:]], axis=1)


def unpack(values):
    count, rows, _ = values.shape
    halves = [values[:, :, :64], values[:, :, 64:]]
    return jnp.stack(halves, axis=1).reshape(count * rows * 2, 64)


def right_kernel(rows, right, out):
    turned = fold(dot(split(rows[...], 0), right[...], 1, 0))
    for r in range(16):
        zl, yx = r // 8, r % 8
        for b in range(4):
            piece = turned[16 * b : 16 * b + 16, 64 * r : 64 * r + 64]
            out[yx * 8 + b * 2 + zl] = pack(piece)


def left_kernel(turned, left, moment, second, rotated, out):
    spun = fold(dot(split(unpack(turned[...]), 1), left[...], 0, 0))
    rotated[...] = spun
    normed = adam_step(moment[...], second[...], spun)[2]
    back = fold(dot(split(normed, 0), left[...], 1, 1))
    for r in range(16):
        out[r] = pack(back[:, 64 * r : 64 * r + 64])


def weight_kernel(back, right, weight, new_weight, update):
    unrotated = fold(dot(split(unpack(back[...]), 1), right[...], 0, 1))
    old = weight[...]
    new_weight[...] = old - learn_rate * (unrotated + weight_decay * old)
    update[...] = unrotated.astype(BF16)


def call(kernel, outs, *args, flops):
    vmem = pl.BlockSpec(memory_space=pltpu.VMEM)
    moved = sum(a.size * a.dtype.itemsize for a in args)
    return pl.pallas_call(
        kernel,
        out_shape=[jax.ShapeDtypeStruct(shape, dtype) for shape, dtype in outs],
        in_specs=[vmem] * len(args),
        out_specs=[vmem] * len(outs),
        compiler_params=pltpu.CompilerParams(vmem_limit_bytes=40 << 20),
        cost_estimate=pl.CostEstimate(flops=flops, bytes_accessed=moved, transcendentals=0),
    )(*args)


def after(values, earlier):
    return lax.optimization_barrier((values, earlier))[0]


def ring_sum(parts, axes, count, dim, up, seen=None):
    here = lax.axis_index(axes)

    def block(offset):
        return lax.dynamic_index_in_dim(parts, (here + offset) % count, dim, keepdims=False)

    down = count - 1 - up
    from_below, from_above = block(up), block(-down)
    for step in range(max(up, down)):
        if step < up:
            from_below = shift(from_below, axes, count, 1)
            if step < up - 1:
                from_below = from_below + block(up - 1 - step)
                if seen is not None:
                    seen.append(from_below)
        if step < down:
            from_above = shift(from_above, axes, count, -1)
            if step < down - 1:
                from_above = from_above + block(-(down - 1 - step))
    return block(0) + from_below + from_above if down else block(0) + from_below


def local(attn_out, out_grad, q_left, q_right, weight, moment, second):
    yl, yh, core = (lax.axis_index(a) for a in ("yl", "yh", "core"))

    half = out_grad.shape[1] // 2
    mine = lax.dynamic_slice_in_dim(out_grad, yl * half, half, 1)
    others = lax.dynamic_slice_in_dim(out_grad, (1 - yl) * half, half, 1)
    grad_1 = swap(out_grad, "core")
    grad_2 = swap(mine, "yh")
    grad_2y = lax.ppermute(others, ("yh", "yl"), [(i, 3 - i) for i in range(4)])
    attn_y = swap(attn_out, "yl")

    part_0 = dot(out_grad, attn_out, 0, 0).reshape(2, 4, 128, 1024)
    part_1 = dot(grad_1, attn_out, 0, 0).reshape(2, 4, 8, 16, 1024)
    seen_0, seen_1 = [], []
    sum_0 = ring_sum(part_0, "x", 4, 1, 2, seen_0).reshape(2, 8, 16, 1024)
    sum_1 = ring_sum(part_1, Z, 8, 2, 4, seen_1)

    right = q_right[0].reshape(16, 4, 16, 16).transpose(0, 2, 1, 3).reshape(1, 16, 1024)
    bases = jnp.concatenate([q_left[0], jnp.broadcast_to(right, (4, 16, 1024))], axis=1)
    bases = lax.all_to_all(after(bases, part_1), "zh", 0, 0, tiled=True)
    moved = jnp.stack([moment, second]).reshape(2, 16, 4, 1024).transpose(2, 0, 1, 3)
    moved = lax.all_to_all(after(moved, bases), "zh", 0, 0, tiled=True)
    bases = pair(bases, "zl")
    bases = lax.all_gather(bases, "x", axis=0).reshape(4, 2, 4, 2, 16, 1024)
    right = pair(bases[:, :, :, 1], "yl")
    left = pair(after(bases[:, :, :, 0], right), "yl")

    grad_2, grad_2y, attn_y = after((grad_2, grad_2y, attn_y), (seen_0[0], seen_1[0]))
    grad_3, grad_3y = swap(grad_2, "core"), swap(grad_2y, "core")
    part_2 = dot(grad_2, attn_out, 0, 0) + dot(grad_2y, attn_y, 0, 0)
    part_3 = dot(grad_3, attn_out, 0, 0) + dot(grad_3y, attn_y, 0, 0)
    sum_2 = ring_sum(part_2.reshape(4, 128, 1024), "x", 4, 0, 2)
    sum_3 = ring_sum(part_3.reshape(4, 128, 1024), "x", 4, 0, 1)

    sum_0 = ring_sum(sum_0, "yl", 2, 0, 1)
    sum_1 = ring_sum(ring_sum(sum_1, "yl", 2, 0, 1), "x", 4, 0, 1)
    rest = jnp.stack([sum_0.reshape(128, 1024), sum_2, sum_3]).reshape(3, 8, 16, 1024)
    rest, moved, right = lax.optimization_barrier((rest, moved, right))
    right, left = (b.transpose(3, 2, 0, 1, 4, 5).reshape(1024, 1024) for b in (right, left))
    moment_b, second_b = (moved[:, i].reshape(64, 1024) for i in (0, 1))
    row_0, row_2, row_3 = ring_sum(rest, Z, 8, 1, 4)
    rows_a, rows_b = jnp.stack([row_0, sum_1]), jnp.stack([row_2, row_3])
    rows_a = jnp.where(core == 1, rows_a[::-1], rows_a)
    rows_b = jnp.where(core == 1, rows_b[::-1], rows_b)
    rows = jnp.concatenate(
        [jnp.where(yh == 1, rows_b, rows_a), jnp.where(yh == 1, rows_a, rows_b)]
    ).reshape(64, 1024)

    flops = 2 * 128 * 1024 * 1024
    (turned,) = call(right_kernel, [((64, 8, 128), F32)], rows, right, flops=flops)
    turned = lax.all_to_all(turned, ("yl", "x", "zh", "zl"), 0, 0, tiled=True)
    rotated, back = call(
        left_kernel,
        [((64, 1024), F32), ((16, 32, 128), F32)],
        turned, left, moment_b, second_b,
        flops=2 * flops,
    )
    back = lax.all_to_all(back, ("zl", "yl", "x"), 0, 0, tiled=True)
    new_weight, update = call(
        weight_kernel,
        [((64, 1024), F32), ((64, 1024), BF16)],
        back, right, weight,
        flops=flops,
    )

    zh = lax.axis_index("zh")
    tiles = rotated.reshape(4, 16, 1024)
    own = jnp.zeros((4, 16, 1024), F32)
    for step in range(4):
        sent = lax.dynamic_index_in_dim(tiles, (zh + step) % 4, 0, keepdims=False)
        got = shift(sent, "zh", 4, step) if step else sent
        own = lax.dynamic_update_index_in_dim(own, got, (zh - step) % 4, 0)
    own = own.transpose(1, 0, 2).reshape(16, 4096)
    new_moment, new_second, _ = adam_step(moment, second, own)
    return (new_weight, update, new_moment, new_second)


def solution(mesh):
    fine = Mesh(mesh.devices.reshape(tuple(SIZES.values())), tuple(SIZES))
    tensor, dp = ("yh", "core"), ("zh", "zl", "yl", "x")
    whole = tensor + dp
    return jax.shard_map(
        local,
        mesh=fine,
        in_specs=(
            P(dp, tensor),
            P(dp, tensor),
            P(tensor, None, dp, None),
            P(tensor, dp, None),
            P(dp, tensor),
            P(whole, None),
            P(whole, None),
        ),
        out_specs=(P(dp, tensor), P(dp, tensor), P(whole, None), P(whole, None)),
        check_vma=False,
    )
```

```python
import jax
import jax.numpy as jnp
from jax import lax
from jax.experimental import pallas as pl
from jax.experimental.pallas import tpu as pltpu
from jax.sharding import Mesh, PartitionSpec as P

STEP = 10


beta_first = 0.9
beta_second = 0.95
adam_eps = 1e-08
learn_rate = 0.1
weight_decay = 0.1

SIZES = {"yh": 2, "core": 2, "zh": 4, "zl": 2, "yl": 2, "x": 4}
Z = ("zh", "zl")
F32, BF16 = jnp.float32, jnp.bfloat16


def adam_step(moment, second, rotated):
    new_moment = beta_first * moment + (1.0 - beta_first) * rotated
    new_second = beta_second * second + (1.0 - beta_second) * rotated * rotated
    first_fix = 1.0 - beta_first**STEP
    second_fix = 1.0 - beta_second**STEP
    normed = new_moment / first_fix / (jnp.sqrt(new_second / second_fix) + adam_eps)
    return (new_moment, new_second, normed)


def shift(value, axes, count, by):
    return lax.ppermute(value, axes, [(i, (i + by) % count) for i in range(count)])


def swap(value, axis):
    return shift(value, axis, 2, 1)


def pair(value, axis):
    other, first = swap(value, axis), lax.axis_index(axis) == 0
    return jnp.stack([jnp.where(first, value, other), jnp.where(first, other, value)])


def split(value, dim):
    high = value.astype(BF16)
    low = (value - high.astype(F32)).astype(BF16)
    return jnp.concatenate([high, low], axis=dim)


def fold(value):
    half = value.shape[0] // 2
    return value[:half] + value[half:]


def dot(left, right, left_dim, right_dim):
    return lax.dot_general(
        left, right, (((left_dim,), (right_dim,)), ((), ())), preferred_element_type=F32
    )


def pack(value):
    half = value.shape[0] // 2
    return jnp.concatenate([value[:half], value[half:]], axis=1)


def unpack(values):
    count, rows, _ = values.shape
    halves = [values[:, :, :64], values[:, :, 64:]]
    return jnp.stack(halves, axis=1).reshape(count * rows * 2, 64)


def right_kernel(rows, right, out):
    turned = fold(dot(split(rows[...], 0), right[...], 1, 0))
    for r in range(16):
        zl, yx = r // 8, r % 8
        for b in range(4):
            piece = turned[16 * b : 16 * b + 16, 64 * r : 64 * r + 64]
            out[yx * 8 + b * 2 + zl] = pack(piece)


def left_kernel(turned, left, moment, second, rotated, out):
    spun = fold(dot(split(unpack(turned[...]), 1), left[...], 0, 0))
    rotated[...] = spun
    normed = adam_step(moment[...], second[...], spun)[2]
    back = fold(dot(split(normed, 0), left[...], 1, 1))
    for r in range(16):
        out[r] = pack(back[:, 64 * r : 64 * r + 64])


def weight_kernel(back, right, weight, new_weight, update):
    unrotated = fold(dot(split(unpack(back[...]), 1), right[...], 0, 1))
    old = weight[...]
    new_weight[...] = old - learn_rate * (unrotated + weight_decay * old)
    update[...] = unrotated.astype(BF16)


def call(kernel, outs, *args, flops):
    vmem = pl.BlockSpec(memory_space=pltpu.VMEM)
    moved = sum(a.size * a.dtype.itemsize for a in args)
    return pl.pallas_call(
        kernel,
        out_shape=[jax.ShapeDtypeStruct(shape, dtype) for shape, dtype in outs],
        in_specs=[vmem] * len(args),
        out_specs=[vmem] * len(outs),
        compiler_params=pltpu.CompilerParams(vmem_limit_bytes=14 << 20),
        cost_estimate=pl.CostEstimate(flops=flops, bytes_accessed=moved, transcendentals=0),
    )(*args)


def after(values, earlier):
    return lax.optimization_barrier((values, earlier))[0]


def ring_sum(parts, axes, count, dim, up, seen=None):
    here = lax.axis_index(axes)

    def block(offset):
        return lax.dynamic_index_in_dim(parts, (here + offset) % count, dim, keepdims=False)

    down = count - 1 - up
    from_below, from_above = block(up), block(-down)
    for step in range(max(up, down)):
        if step < up:
            from_below = shift(from_below, axes, count, 1)
            if step < up - 1:
                from_below = from_below + block(up - 1 - step)
                if seen is not None:
                    seen.append(from_below)
        if step < down:
            from_above = shift(from_above, axes, count, -1)
            if step < down - 1:
                from_above = from_above + block(-(down - 1 - step))
    return block(0) + from_below + from_above if down else block(0) + from_below


def local(attn_out, out_grad, q_left, q_right, weight, moment, second):
    yl, yh, core = (lax.axis_index(a) for a in ("yl", "yh", "core"))

    half = out_grad.shape[1] // 2
    mine = lax.dynamic_slice_in_dim(out_grad, yl * half, half, 1)
    others = lax.dynamic_slice_in_dim(out_grad, (1 - yl) * half, half, 1)
    grad_1 = swap(out_grad, "core")
    grad_2 = swap(mine, "yh")
    grad_2y = lax.ppermute(others, ("yh", "yl"), [(i, 3 - i) for i in range(4)])
    attn_y = swap(attn_out, "yl")

    part_0 = dot(out_grad, attn_out, 0, 0).reshape(2, 4, 128, 1024)
    part_1 = dot(grad_1, attn_out, 0, 0).reshape(2, 4, 8, 16, 1024)
    seen_0, seen_1 = [], []
    sum_0 = ring_sum(part_0, "x", 4, 1, 2, seen_0).reshape(2, 8, 16, 1024)
    sum_1 = ring_sum(part_1, Z, 8, 2, 4, seen_1)

    right = q_right[0].reshape(16, 4, 16, 16).transpose(0, 2, 1, 3).reshape(1, 16, 1024)
    bases = jnp.concatenate([q_left[0], jnp.broadcast_to(right, (4, 16, 1024))], axis=1)
    bases = lax.all_to_all(after(bases, part_1), "zh", 0, 0, tiled=True)
    moved = jnp.stack([moment, second]).reshape(2, 16, 4, 1024).transpose(2, 0, 1, 3)
    moved = lax.all_to_all(after(moved, bases), "zh", 0, 0, tiled=True)
    bases = pair(bases, "zl")
    bases = lax.all_gather(bases, "x", axis=0).reshape(4, 2, 4, 2, 16, 1024)
    right = pair(bases[:, :, :, 1], "yl")
    left = pair(after(bases[:, :, :, 0], right), "yl")

    grad_2, grad_2y, attn_y = after((grad_2, grad_2y, attn_y), (seen_0[0], seen_1[0]))
    grad_3, grad_3y = swap(grad_2, "core"), swap(grad_2y, "core")
    part_2 = dot(grad_2, attn_out, 0, 0) + dot(grad_2y, attn_y, 0, 0)
    part_3 = dot(grad_3, attn_out, 0, 0) + dot(grad_3y, attn_y, 0, 0)
    sum_2 = ring_sum(part_2.reshape(4, 128, 1024), "x", 4, 0, 2)
    sum_3 = ring_sum(part_3.reshape(4, 128, 1024), "x", 4, 0, 1)

    sum_0 = ring_sum(sum_0, "yl", 2, 0, 1)
    sum_1 = ring_sum(ring_sum(sum_1, "yl", 2, 0, 1), "x", 4, 0, 1)
    rest = jnp.stack([sum_0.reshape(128, 1024), sum_2, sum_3]).reshape(3, 8, 16, 1024)
    rest, moved, right = lax.optimization_barrier((rest, moved, right))
    right, left = (b.transpose(3, 2, 0, 1, 4, 5).reshape(1024, 1024) for b in (right, left))
    moment_b, second_b = (moved[:, i].reshape(64, 1024) for i in (0, 1))
    row_0, row_2, row_3 = ring_sum(rest, Z, 8, 1, 4)
    rows_a, rows_b = jnp.stack([row_0, sum_1]), jnp.stack([row_2, row_3])
    rows_a = jnp.where(core == 1, rows_a[::-1], rows_a)
    rows_b = jnp.where(core == 1, rows_b[::-1], rows_b)
    rows = jnp.concatenate(
        [jnp.where(yh == 1, rows_b, rows_a), jnp.where(yh == 1, rows_a, rows_b)]
    ).reshape(64, 1024)

    flops = 2 * 128 * 1024 * 1024
    (turned,) = call(right_kernel, [((64, 8, 128), F32)], rows, right, flops=flops)
    turned = lax.all_to_all(turned, ("yl", "x", "zh", "zl"), 0, 0, tiled=True)
    rotated, back = call(
        left_kernel,
        [((64, 1024), F32), ((16, 32, 128), F32)],
        turned, left, moment_b, second_b,
        flops=2 * flops,
    )
    back = lax.all_to_all(back, ("zl", "yl", "x"), 0, 0, tiled=True)
    new_weight, update = call(
        weight_kernel,
        [((64, 1024), F32), ((64, 1024), BF16)],
        back, right, weight,
        flops=flops,
    )

    zh = lax.axis_index("zh")
    tiles = rotated.reshape(4, 16, 1024)
    own = jnp.zeros((4, 16, 1024), F32)
    for step in range(4):
        sent = lax.dynamic_index_in_dim(tiles, (zh + step) % 4, 0, keepdims=False)
        got = shift(sent, "zh", 4, step) if step else sent
        own = lax.dynamic_update_index_in_dim(own, got, (zh - step) % 4, 0)
    own = own.transpose(1, 0, 2).reshape(16, 4096)
    new_moment, new_second, _ = adam_step(moment, second, own)
    return (new_weight, update, new_moment, new_second)


def solution(mesh):
    fine = Mesh(mesh.devices.reshape(tuple(SIZES.values())), tuple(SIZES))
    tensor, dp = ("yh", "core"), ("zh", "zl", "yl", "x")
    whole = tensor + dp
    return jax.shard_map(
        local,
        mesh=fine,
        in_specs=(
            P(dp, tensor),
            P(dp, tensor),
            P(tensor, None, dp, None),
            P(tensor, dp, None),
            P(dp, tensor),
            P(whole, None),
            P(whole, None),
        ),
        out_specs=(P(dp, tensor), P(dp, tensor), P(whole, None), P(whole, None)),
        check_vma=False,
    )
```
